128 devices in a mesh: face: 4 (over z), tile: 32 (over y, x, core).
Axes of the slice: x: 4, y: 4, z: 4, core: 2. Of those that a mesh axis runs over, the one named last changes fastest.
Arguments:
- profiles: bfloat16 [131072, 2048], P(('face', 'tile'))
- sun_cos: bfloat16 [131072], P(('face', 'tile')), may hold values from 0.049804688 to 1
- albedo: bfloat16 [131072], P(('face', 'tile')), may hold values from 0.049804688 to 0.796875
- span_order: int32 [128, 1024], P(('face', 'tile')), may hold values from 0 to 1023, as said below
- keep_list: int32 [128, 384], P(('face', 'tile')), may hold values from 0 to 1023, as said below
- ship_list: int32 [128, 128], P(('face', 'tile')), may hold values from 0 to 1023, as said below
- ship_count: int32 [128], P(('face', 'tile')), may hold values from 0 to 128, as said below
- w_hidden: bfloat16 [32, 128], replicated, may hold values from -1 to 1
- optical_weight: bfloat16 [128, 336], replicated, may hold values from -0.5 to 0.5
- solar_weight: float32 [112], replicated, may hold values from 0.005 to 0.05
Outputs:
- heating: float32 [64, 131072], P(None, ('face', 'tile'))
- surface_down: float32 [131072], P(('face', 'tile'))
The draws below stay inside these ranges and needn't reach their ends.
Inputs may be any that keep to these rules, and one draw needn't show every extreme that they name: `span_order`: each row is a permutation of the device's 1024 local column slots. `keep_list`: row e names distinct span slots of device e, none of them in row e of ship_list. `ship_list`: row e names distinct span slots of device e, none of them in row e of keep_list. `ship_count`: some device has exactly 128.
All inputs are finite; a program needn't handle non-finite values.
Results may differ from the reference program's by a relative error of at most 0.00052.
Values may be sent and summed in bfloat16 or wider, within the bound.
A program may use at most 192 MiB of HBM per device.

```python
import math
import jax
import jax.numpy as jnp
from jax import lax

L = 64
F = 32
H = 128
G = 112
COLS_DEV = 1024
NDEV = 128
COLUMNS = 131072
KEEP = 384
SHIP = 128


def draw_plan(key):
    base = jax.random.fold_in(key, 7)
    order_keys = jax.random.split(jax.random.fold_in(base, 1), NDEV)
    slot_permutation = jax.vmap(lambda one_key: jax.random.permutation(one_key, COLS_DEV))(order_keys).astype(jnp.int32)
    lit_count = jax.random.randint(jax.random.fold_in(base, 2), (NDEV,), 0, COLS_DEV + 1)
    picked = jax.random.permutation(jax.random.fold_in(base, 3), NDEV)
    lit_count = lit_count.at[picked[:4]].set(COLS_DEV).at[picked[4:8]].set(0)
    per_peer = COLS_DEV // NDEV
    slot_index = jnp.arange(COLS_DEV, dtype=jnp.int32)
    source = slot_index // per_peer
    owner_row = jnp.arange(NDEV, dtype=jnp.int32)[:, None]
    local_slot = slot_permutation[source[None, :], owner_row * per_peer + (slot_index % per_peer)[None, :]]
    sunlit = local_slot < lit_count[source][None, :]
    ranking_random_keys = jax.random.split(jax.random.fold_in(base, 4), NDEV)
    shuffle = jax.vmap(lambda one_key: jax.random.permutation(one_key, COLS_DEV))(ranking_random_keys)
    scores = jnp.where(sunlit, 0, COLS_DEV) + shuffle
    ranking = jnp.argsort(scores, axis=1, stable=True).astype(jnp.int32)
    keep_slots = ranking[:, :KEEP]
    ship_slots = ranking[:, KEEP:KEEP + SHIP]
    lit_total = jnp.sum(sunlit.astype(jnp.int32), axis=1)
    ship_total = jnp.clip(lit_total - KEEP, 0, SHIP)
    forced = jax.random.randint(jax.random.fold_in(base, 5), (), 0, NDEV)
    ship_total = ship_total.at[forced].set(SHIP).astype(jnp.int32)
    return (slot_permutation, keep_slots, ship_slots, ship_total)


def draw_span_order(key, part):
    return draw_plan(key)[0]


def draw_keep_list(key, part):
    return draw_plan(key)[1]


def draw_ship_list(key, part):
    return draw_plan(key)[2]


def draw_ship_count(key, part):
    return draw_plan(key)[3]


def draw_profiles(key, part):
    noise_key = jax.random.fold_in(key, 21)
    mass_key = jax.random.fold_in(key, 22)
    values = jax.random.normal(noise_key, (COLUMNS, L, F), jnp.float32)
    layer_mass = jax.random.uniform(mass_key, (COLUMNS, L, 1), jnp.float32, 0.5, 2.0)
    whole = jnp.concatenate([layer_mass, values[:, :, 1:]], axis=2)
    return whole.reshape(COLUMNS, L * F).astype(jnp.bfloat16)


def steps_of(stream_key, dims, cuts, low, top_value):
    loudness, own = 1.0, jax.random.fold_in(stream_key, 6)
    for position, blocks in cuts:
        heights = jnp.exp(jax.random.uniform(jax.random.fold_in(own, position), (blocks,), jnp.float32, low / len(cuts), top_value / len(cuts)))
        loudness = loudness * jnp.repeat(heights, dims[position] // blocks).reshape([-1 if axis == position else 1 for axis in range(len(dims))])
    return loudness


def gaussian(rng, dims, width, bound, kind=jnp.bfloat16):
    array = jax.random.normal(rng, dims, jnp.float32) * width
    return jnp.minimum(jnp.maximum(array, -bound), bound).astype(kind)


def setup_inputs(seed: int = 0) -> dict:
    keys = jax.random.split(jax.random.key(seed), 11)
    profiles = draw_profiles(jax.random.fold_in(keys[10], 71), 0)
    sun_cos = jnp.clip(0.049804688 + 0.9501953 * jax.random.uniform(keys[1], (COLUMNS,), jnp.float32) ** steps_of(keys[1], (COLUMNS,), ((0, 128),), -0.2, 0.2), 0.049804688, 1.0).astype(jnp.bfloat16)
    albedo = jnp.clip(0.049804688 + 0.7470703 * jax.random.uniform(keys[2], (COLUMNS,), jnp.float32) ** steps_of(keys[2], (COLUMNS,), ((0, 128),), -0.2, 0.2), 0.049804688, 0.796875).astype(jnp.bfloat16)
    span_order = draw_span_order(jax.random.fold_in(keys[10], 71), 0)
    keep_list = draw_keep_list(jax.random.fold_in(keys[10], 71), 0)
    ship_list = draw_ship_list(jax.random.fold_in(keys[10], 71), 0)
    ship_count = draw_ship_count(jax.random.fold_in(keys[10], 71), 0)
    w_hidden = gaussian(keys[7], (F, H), F ** -0.5, 1.0)
    optical_weight = gaussian(keys[8], (H, 3 * G), H ** -0.5, 0.5)
    solar_weight = jnp.clip(jnp.exp(jax.random.uniform(keys[9], (G,), jnp.float32, math.log(0.005), math.log(0.05))), 0.005, 0.05)
    return {"profiles": profiles, "sun_cos": sun_cos, "albedo": albedo, "span_order": span_order, "keep_list": keep_list, "ship_list": ship_list, "ship_count": ship_count, "w_hidden": w_hidden, "optical_weight": optical_weight, "solar_weight": solar_weight}


def two_stream(optical_properties, layer_mass, cosine, surface_albedo, solar_weight):
    levels = layer_mass.shape[1]
    gpoints = solar_weight.shape[0]
    depth = 2.0 * layer_mass[:, :, None] * jnp.exp(optical_properties[:, :, :gpoints]) / levels
    single_albedo = 0.98 * jax.nn.sigmoid(optical_properties[:, :, gpoints:2 * gpoints])
    backscatter = 0.5 * (1.0 - 0.8 * jnp.tanh(optical_properties[:, :, 2 * gpoints:]))
    direct_beam = jnp.exp(-depth / cosine[:, None, None])
    reflect = single_albedo * backscatter * (1.0 - direct_beam)
    transmit = direct_beam + single_albedo * (1.0 - backscatter) * (1.0 - direct_beam)
    reflect_levels = jnp.moveaxis(reflect, 1, 0)
    transmit_levels = jnp.moveaxis(transmit, 1, 0)

    def upward(reflectance_lower, layer_pair):
        reflect_here, transmit_here = layer_pair
        denominator = 1.0 - reflect_here * reflectance_lower
        reflectance_upper = reflect_here + transmit_here * transmit_here * reflectance_lower / denominator
        return reflectance_upper, (reflectance_upper, transmit_here / denominator)

    ground = jnp.broadcast_to(surface_albedo[:, None], (cosine.shape[0], gpoints))
    top_reflect, stacks = lax.scan(upward, ground, (reflect_levels, transmit_levels), reverse=True)

    def downward(flux_down, layer_pair):
        reflect_here, factor_here = layer_pair
        net_flux = jnp.sum(flux_down * (1.0 - reflect_here), axis=1)
        return flux_down * factor_here, net_flux

    incident = cosine[:, None] * solar_weight[None, :]
    bottom_flux, net_levels = lax.scan(downward, incident, stacks)
    net_ground = jnp.sum(bottom_flux * (1.0 - surface_albedo[:, None]), axis=1)
    net_all = jnp.concatenate([net_levels, net_ground[None, :]], axis=0)
    heating_rates = levels * (net_all[:-1] - net_all[1:]) / layer_mass.T
    return heating_rates.T, jnp.sum(bottom_flux, axis=1)


def optics_block(profile_rows, cosine_rows, albedo_rows, w_hidden, optical_weight, solar_weight):
    feature_count = w_hidden.shape[0]
    features = profile_rows.reshape(profile_rows.shape[0], -1, feature_count)
    preact = jnp.einsum("clf,fh->clh", features.astype(jnp.float32), w_hidden.astype(jnp.float32))
    hidden_activations = jax.nn.silu(preact).astype(jnp.bfloat16)
    optical_properties = jnp.einsum("rzv,vp->rzp", hidden_activations.astype(jnp.float32), optical_weight.astype(jnp.float32))
    layer_mass = features[:, :, 0].astype(jnp.float32)
    return two_stream(optical_properties, layer_mass, cosine_rows.astype(jnp.float32), albedo_rows.astype(jnp.float32), solar_weight)


def reference(profiles, sun_cos, albedo, span_order, keep_list, ship_list, ship_count, w_hidden, optical_weight, solar_weight):
    per_peer = COLS_DEV // NDEV
    span_slots = jnp.concatenate([keep_list, ship_list], axis=1).astype(jnp.int32)
    ship_live = jnp.arange(SHIP, dtype=jnp.int32)[None, :] < ship_count[:, None]
    live_rows = jnp.concatenate([jnp.ones((NDEV, KEEP), dtype=bool), ship_live], axis=1).reshape(-1)
    source = span_slots // per_peer
    owner_row = jnp.arange(NDEV, dtype=jnp.int32)[:, None]
    local_slot = span_order[source, owner_row * per_peer + span_slots % per_peer].astype(jnp.int32)
    column = (source * COLS_DEV + local_slot).reshape(-1).astype(jnp.int32)
    listed_count = column.shape[0]
    block_size = 128 if listed_count % 128 == 0 else listed_count
    blocks = listed_count // block_size
    packed = (profiles[column].reshape(blocks, block_size, -1), sun_cos[column].reshape(blocks, block_size), albedo[column].reshape(blocks, block_size))

    def one_block(block_data):
        return optics_block(block_data[0], block_data[1], block_data[2], w_hidden, optical_weight, solar_weight)

    heating_rates, surface_flux = lax.map(one_block, packed)
    heating_rates = jnp.where(live_rows[:, None], heating_rates.reshape(listed_count, -1), 0.0)
    surface_flux = jnp.where(live_rows, surface_flux.reshape(listed_count), 0.0)
    heating = jnp.zeros((COLUMNS, L), jnp.float32).at[column].set(heating_rates)
    surface_down = jnp.zeros((COLUMNS,), jnp.float32).at[column].set(surface_flux)
    return heating.T, surface_down
```

```python
import functools, math
import jax, jax.numpy as jnp
from jax import lax
from jax.experimental import pallas as pl
from jax.experimental.pallas import tpu as pltpu
from jax.sharding import PartitionSpec as P

L, F, H, G = 64, 32, 128, 112
LOG2E = math.log2(math.e)
UNROLL = 8
VALUE = True
BFHID = False
SPLIT = 1
GT = 8

def radiate_kernel(prof_ref, cos_ref, alb_ref, wh_ref, wo_ref, sw_ref, heat_ref, surf_ref,
                   whb, wob, swb, hid, mass_s, k_s, opt, t_s, s_s, inv_s, n_s, d_s, net_s):
    C = prof_ref.shape[0]
    @pl.when(pl.program_id(0) == 0)
    def _():
        whb[...] = jnp.zeros_like(whb)
        wt = (wh_ref[...].astype(jnp.float32) * 0.5).T.astype(jnp.bfloat16)
        for j in range(8):
            whb[j*H:(j+1)*H, j*F:(j+1)*F] = wt
        r = lax.broadcasted_iota(jnp.int32, (16, 256), 0)
        c = lax.broadcasted_iota(jnp.int32, (16, 256), 1)
        whb[8*H:8*H+16, :] = jnp.where(c == r * F, 1.0, 0.0).astype(jnp.bfloat16)
        wo = wo_ref[...].astype(jnp.float32).T
        for g in range(0, G, 16):
            wob[3*g:3*g+16] = wo[g:g+16].astype(jnp.bfloat16)
            wob[3*g+16:3*g+32] = (wo[G+g:G+g+16] * 0.5).astype(jnp.bfloat16)
            wob[3*g+32:3*g+48] = wo[2*G+g:2*G+g+16].astype(jnp.bfloat16)
        swb[...] = jnp.broadcast_to(sw_ref[...], (C, G)).T
    cos = cos_ref[...].astype(jnp.float32)
    alb = alb_ref[...].astype(jnp.float32)
    scale = (-2.0 * LOG2E / L) / cos
    n_s[...] = jnp.broadcast_to(alb, (G, C))

    def chunk_body(i, _):
        ch = 7 - i
        x = prof_ref[:, pl.ds(pl.multiple_of(ch * 256, 256), 256)]
        pre = lax.dot_general(whb[...], x, (((1,), (1,)), ((), ())), preferred_element_type=jnp.float32)
        h = pre[:8*H]
        if BFHID:
            hb = h.astype(jnp.bfloat16)
            hid[...] = hb + hb * jnp.tanh(hb)
        else:
            hid[...] = (h + h * jnp.tanh(h)).astype(jnp.bfloat16)
        mass = pre[8*H:8*H+8]
        mass_s[pl.ds(pl.multiple_of(ch * 8, 8), 8), :] = mass
        kk = mass * scale
        for j in range(8):
            k_s[j] = jnp.broadcast_to(kk[j:j+1], (8, C))
        d_s[...] = jnp.ones((G, C), jnp.float32)

        def level(jj):
            l = ch * 8 + jj
            off = jj * H if isinstance(jj, int) else pl.multiple_of(jj * H, H)
            W = C // SPLIT
            for sp in range(SPLIT):
                cs = slice(sp * W, (sp + 1) * W)
                hl = hid[pl.ds(off, H), cs]
                o = jnp.dot(wob[...], hl, preferred_element_type=jnp.float32)
                if not VALUE:
                    opt[:, cs] = o
                    o = opt.at[:, cs]
                kl = k_s[jj, :, cs]
                if GT == 16: kl = jnp.concatenate([kl, kl], axis=0)
                for g in range(0, G, GT):
                    base = 3 * (g // 16) * 16 + g % 16
                    a = o[base:base+GT, :]
                    b = o[base+16:base+16+GT, :]
                    c = o[base+32:base+32+GT, :]
                    D = jnp.exp2(kl * jnp.exp2(a * LOG2E))
                    E = 1.0 - D
                    h2 = (0.245 + 0.245 * jnp.tanh(b)) * E
                    w = h2 * (0.8 * jnp.tanh(c))
                    r = h2 - w
                    t = D + (h2 + w)
                    N = n_s[g:g+GT, cs]
                    Dn = d_s[g:g+GT, cs] - r * N
                    Nn = r * Dn + t * (t * N)
                    n_s[g:g+GT, cs] = Nn
                    d_s[g:g+GT, cs] = Dn
                    t_s[l, g:g+GT, cs] = t
                    s_s[l, g:g+GT, cs] = Dn - Nn
        if UNROLL == 8:
            for jj in range(7, -1, -1): level(jj)
        else:
            def lb(j, _):
                for u in range(UNROLL):
                    level(7 - (j * UNROLL + u))
                return 0
            lax.fori_loop(0, 8 // UNROLL, lb, 0)
        for g in range(0, G, 8):
            inv = pltpu.reciprocal(d_s[g:g+8, :], approx=False)
            inv_s[ch, g:g+8, :] = inv
            n_s[g:g+8, :] = n_s[g:g+8, :] * inv
        return 0
    lax.fori_loop(0, 8, chunk_body, 0)

    W = 128
    for sp in range(C // W):
        cs = slice(sp * W, (sp + 1) * W)
        def down_chunk(ch, down):
            w = [down[i] * inv_s[ch, 8*i:8*i+8, cs] for i in range(G // 8)]
            rows = []
            for j in range(8):
                l = ch * 8 + j
                acc = None
                for i in range(G // 8):
                    p = w[i] * s_s[l, 8*i:8*i+8, cs]
                    acc = p if acc is None else acc + p
                    w[i] = w[i] * t_s[l, 8*i:8*i+8, cs]
                rows.append(jnp.sum(acc, axis=0, keepdims=True))
            net_s[pl.ds(pl.multiple_of(ch * 8, 8), 8), cs] = jnp.concatenate(rows, axis=0)
            return tuple(w)
        down = lax.fori_loop(0, 8, down_chunk, tuple(swb[g:g+8, cs] * cos[:, cs] for g in range(0, G, 8)))
        acc = down[0]
        for g in range(1, G//8):
            acc = acc + down[g]
        surf = jnp.sum(acc, axis=0, keepdims=True)
        surf_ref[:, cs] = surf
        net_s[L:L+1, cs] = surf * (1.0 - alb[:, cs])
    heat_ref[...] = L * (net_s[0:L, :] - net_s[1:L+1, :]) / mass_s[...]

def radiate(prof, cos, alb, wh, wo, sw, C=256):
    N = prof.shape[0]
    grid = (N // C,)
    full = lambda s: pl.BlockSpec(s, lambda i: (0,) * len(s))
    return pl.pallas_call(
        radiate_kernel,
        grid=grid,
        in_specs=[pl.BlockSpec((C, L*F), lambda i: (i, 0)),
                  pl.BlockSpec((1, C), lambda i: (0, i)),
                  pl.BlockSpec((1, C), lambda i: (0, i)),
                  full((F, H)), full((H, 3*G)), full((1, G))],
        out_specs=[pl.BlockSpec((L, C), lambda i: (0, i)), pl.BlockSpec((1, C), lambda i: (0, i))],
        out_shape=[jax.ShapeDtypeStruct((L, N), jnp.float32), jax.ShapeDtypeStruct((1, N), jnp.float32)],
        scratch_shapes=[pltpu.VMEM((8*H+16, 256), jnp.bfloat16), pltpu.VMEM((3*G, H), jnp.bfloat16), pltpu.VMEM((G, C), jnp.float32),
                        pltpu.VMEM((8*H, C), jnp.bfloat16), pltpu.VMEM((L, C), jnp.float32), pltpu.VMEM((8, 8, C), jnp.float32),
                        pltpu.VMEM((3*G, C), jnp.float32), pltpu.VMEM((L, G, C), jnp.float32), pltpu.VMEM((L, G, C), jnp.float32),
                        pltpu.VMEM((8, G, C), jnp.float32), pltpu.VMEM((G, C), jnp.float32), pltpu.VMEM((G, C), jnp.float32),
                        pltpu.VMEM((L+8, C), jnp.float32)],
        compiler_params=pltpu.CompilerParams(vmem_limit_bytes=60*2**20),
        cost_estimate=pl.CostEstimate(flops=6*10**9, bytes_accessed=2**23, transcendentals=4*10**7),
    )(prof, cos.reshape(1, N), alb.reshape(1, N), wh, wo, sw.reshape(1, G))


def mask_kernel(lists_ref, order_ref, raw_heat_ref, raw_surf_ref, heat_ref, surf_ref):
    devices, entries = lists_ref.shape
    columns = order_ref.shape[1]
    per_peer = columns // devices
    me = lax.axis_index("face") * lax.axis_size("tile") + lax.axis_index("tile")
    lists = lists_ref[...]
    ones = jnp.ones((8, entries), jnp.bfloat16)
    one_hot = lambda hit: jnp.where(hit, 1.0, 0.0).astype(jnp.bfloat16)
    contract_lanes = (((1,), (1,)), ((), ()))
    rows = []
    for k in range(per_peer):
        hit = one_hot(lists == me * per_peer + k)
        rows.append(lax.dot_general(ones, hit, contract_lanes, preferred_element_type=jnp.float32)[0:1])
    flags = jnp.concatenate(rows, axis=0)
    slot = lax.broadcasted_iota(jnp.int32, (devices, columns), 1)
    peer = lax.broadcasted_iota(jnp.int32, (devices, columns), 0)
    spread = jnp.dot(flags.astype(jnp.bfloat16), one_hot(slot // per_peer == peer), preferred_element_type=jnp.float32)
    share = lax.broadcasted_iota(jnp.int32, (per_peer, columns), 0)
    at = lax.broadcasted_iota(jnp.int32, (per_peer, columns), 1)
    flag = jnp.sum(jnp.where(at % per_peer == share, spread, 0.0), axis=0, keepdims=True)
    order = order_ref[...]
    group = lax.broadcasted_iota(jnp.int32, (columns // 128, columns), 0)
    lane = lax.broadcasted_iota(jnp.int32, (128, columns), 0)
    left = jnp.where(order // 128 == group, flag, 0.0).astype(jnp.bfloat16)
    listed = lax.dot_general(left, one_hot(order % 128 == lane), contract_lanes, preferred_element_type=jnp.float32)
    for i in range(columns // 128):
        cs = slice(i * 128, (i + 1) * 128)
        live = listed[i : i + 1, :] > 0.5
        heat_ref[:, cs] = jnp.where(live, raw_heat_ref[:, cs], 0.0)
        surf_ref[:, cs] = jnp.where(live, raw_surf_ref[:, cs], 0.0)


def on_device(profiles, sun_cos, albedo, span_order, keep_list, ship_list, ship_count, w_hidden, optical_weight, solar_weight):
    ship_live = jnp.arange(ship_list.shape[1])[None, :] < ship_count[:, None]
    named = jnp.concatenate([keep_list, jnp.where(ship_live, ship_list, -1)], axis=1)
    lists = lax.all_gather(named, ("face", "tile"), axis=0, tiled=True)
    raw_heat, raw_surf = radiate(profiles, sun_cos, albedo, w_hidden, optical_weight, solar_weight)
    heat, surf = pl.pallas_call(
        mask_kernel,
        out_shape=[jax.ShapeDtypeStruct(raw_heat.shape, jnp.float32), jax.ShapeDtypeStruct(raw_surf.shape, jnp.float32)],
        cost_estimate=pl.CostEstimate(flops=2**23, bytes_accessed=2**20, transcendentals=0),
    )(lists, span_order, raw_heat, raw_surf)
    return heat, surf.reshape(-1)


def solution(mesh):
    both = ("face", "tile")
    rows, flat = P(both, None), P(both)
    placed = (rows, flat, flat, rows, rows, rows, flat, P(), P(), P())
    return jax.shard_map(on_device, mesh=mesh, in_specs=placed, out_specs=(P(None, both), flat), check_vma=False)
```

```python
import functools, math
import jax, jax.numpy as jnp
from jax import lax
from jax.experimental import pallas as pl
from jax.experimental.pallas import tpu as pltpu
from jax.sharding import PartitionSpec as P

L, F, H, G = 64, 32, 128, 112
LOG2E = math.log2(math.e)
U = 4
W = 256
DU = 1
ORDER = 0
NODOT = False
STAGE = False
XT = 0
NH = 8
NG = 8
ND = 8
DFIRST = False
RENORM = 8

def radiate_kernel(prof_ref, cos_ref, alb_ref, wh_ref, wo_ref, sw_ref, heat_ref, surf_ref,
                   whb, wob, swb, hid, mass_s, k_s, opt, t_s, s_s, inv_s, n_s, d_s, net_s):
    C = prof_ref.shape[0]
    @pl.when(pl.program_id(0) == 0)
    def _():
        whb[...] = jnp.zeros_like(whb)
        wt = (wh_ref[...].astype(jnp.float32) * 0.5).T.astype(jnp.bfloat16)
        for j in range(8):
            whb[j*H:(j+1)*H, j*F:(j+1)*F] = wt
        r = lax.broadcasted_iota(jnp.int32, (16, 256), 0)
        c = lax.broadcasted_iota(jnp.int32, (16, 256), 1)
        whb[8*H:8*H+16, :] = jnp.where(c == r * F, 1.0, 0.0).astype(jnp.bfloat16)
        for g in range(0, G, 16):
            wob[3*g:3*g+16] = wo_ref[g:g+16]
            wob[3*g+16:3*g+32] = (wo_ref[G+g:G+g+16].astype(jnp.float32) * 0.5).astype(jnp.bfloat16)
            wob[3*g+32:3*g+48] = wo_ref[2*G+g:2*G+g+16]
        swb[...] = jnp.broadcast_to(sw_ref[...], (128, G)).T
    cos = cos_ref[...].astype(jnp.float32)
    alb = alb_ref[...].astype(jnp.float32)
    scale = (-2.0 * LOG2E / L) / cos
    n_s[...] = jnp.broadcast_to(alb, (G, C))

    def hidden_chunk(ch, _):
        k0 = pl.multiple_of(ch * 256, 256)
        for s in range(C // W):
            cs = slice(s * W, (s + 1) * W)
            x = prof_ref[cs, pl.ds(k0, 256)]
            if XT == 0:
                pre = lax.dot_general(whb[...], x, (((1,), (1,)), ((), ())), preferred_element_type=jnp.float32)
            elif XT == 1:
                pre = jnp.dot(whb[...], x.T, preferred_element_type=jnp.float32)
            elif XT == 2:
                pre = jnp.dot(whb[...], x.astype(jnp.float32).T.astype(jnp.bfloat16), preferred_element_type=jnp.float32)
            h = pre[:8*H]
            hid[pl.ds(pl.multiple_of(ch * 8 * H, 8 * H), 8 * H), cs] = (h + h * jnp.tanh(h)).astype(jnp.bfloat16)
            mass = pre[8*H:8*H+8]
            mass_s[pl.ds(pl.multiple_of(ch * 8, 8), 8), cs] = mass
            kk = mass * scale[:, cs]
            for j in range(8):
                k_s[ch * 8 + j, :, cs] = jnp.broadcast_to(kk[j:j+1], (8, W))
        return 0
    lax.fori_loop(0, NH, hidden_chunk, 0)

    def dots(l, p):
        for u in range(U):
            for s in range(C // W):
                cs = slice(s * W, (s + 1) * W)
                lu = jnp.maximum(l - u, 0)
                opt[p, u, :, cs] = jnp.dot(wob[...], hid[pl.ds(pl.multiple_of(lu * H, H), H), cs], preferred_element_type=jnp.float32)

    def elem(l, p):
        for s in range(C // 128):
            cs = slice(s * 128, (s + 1) * 128)
            for g in range(0, G, 8):
                base = 3 * (g // 16) * 16 + g % 16
                N = n_s[g:g+8, cs]
                Dn = d_s[g:g+8, cs]
                for u in range(U):
                    a = opt[p, u, base:base+8, cs]
                    b = opt[p, u, base+16:base+24, cs]
                    c = opt[p, u, base+32:base+40, cs]
                    D = jnp.exp2(k_s[l - u, :, cs] * jnp.exp2(a * LOG2E))
                    E = 1.0 - D
                    h2 = (0.245 + 0.245 * jnp.tanh(b)) * E
                    w = h2 * (0.8 * jnp.tanh(c))
                    r = h2 - w
                    t = D + (h2 + w)
                    Dn = Dn - r * N
                    N = r * Dn + t * (t * N)
                    t_s[l - u, g:g+8, cs] = t
                    s_s[l - u, g:g+8, cs] = Dn - N
                n_s[g:g+8, cs] = N
                d_s[g:g+8, cs] = Dn

    dots(L - 1, 0)
    def group(i, _):
        l0 = L - 1 - i * RENORM
        d_s[...] = jnp.ones((G, C), jnp.float32)
        def inner(j, _):
            l = l0 - U * j
            for p in (0, 1):
                @pl.when(lax.rem(j, 2) == p)
                def _():
                    if DFIRST:
                        NODOT or dots(l - U, 1 - p)
                        elem(l, p)
                    else:
                        elem(l, p)
                        NODOT or dots(l - U, 1 - p)
            return 0
        lax.fori_loop(0, RENORM // U, inner, 0)
        ch = L // RENORM - 1 - i
        for g in range(0, G, 8):
            inv = pltpu.reciprocal(d_s[g:g+8, :], approx=False)
            inv_s[ch, g:g+8, :] = inv
            n_s[g:g+8, :] = n_s[g:g+8, :] * inv
        return 0
    lax.fori_loop(0, NG * (8 // RENORM), group, 0)

    V = 128
    for sp in range(C // V):
        cs = slice(sp * V, (sp + 1) * V)
        def down_chunk(ch, down):
            w = list(down)
            rows = []
            for j in range(8):
                l = ch * 8 + j
                if j % RENORM == 0:
                    ii = ch if RENORM == 8 else ch * (8 // RENORM) + j // RENORM
                    w = [w[i] * inv_s[ii, 8*i:8*i+8, cs] for i in range(G // 8)]
                acc = None
                for i in range(G // 8):
                    p = w[i] * s_s[l, 8*i:8*i+8, cs]
                    acc = p if acc is None else acc + p
                    w[i] = w[i] * t_s[l, 8*i:8*i+8, cs]
                rows.append(jnp.sum(acc, axis=0, keepdims=True))
            net_s[pl.ds(pl.multiple_of(ch * 8, 8), 8), cs] = jnp.concatenate(rows, axis=0)
            return tuple(w)
        down = lax.fori_loop(0, ND, down_chunk, tuple(swb[g:g+8, :] * cos[:, cs] for g in range(0, G, 8)))
        acc = down[0]
        for g in range(1, G//8):
            acc = acc + down[g]
        surf = jnp.sum(acc, axis=0, keepdims=True)
        surf_ref[:, cs] = surf
        net_s[L:L+1, cs] = surf * (1.0 - alb[:, cs])
    heat_ref[...] = L * (net_s[0:L, :] - net_s[1:L+1, :]) / mass_s[...]

def radiate(prof, cos, alb, wh, wo, sw, C=256):
    N = prof.shape[0]
    grid = (N // C,)
    full = lambda s: pl.BlockSpec(s, lambda i: (0,) * len(s))
    vm = lambda *s: pltpu.VMEM(s, jnp.float32)
    vb = lambda *s: pltpu.VMEM(s, jnp.bfloat16)
    return pl.pallas_call(
        radiate_kernel,
        grid=grid,
        in_specs=[pl.BlockSpec((C, L*F), lambda i: (i, 0)),
                  pl.BlockSpec((1, C), lambda i: (0, i)),
                  pl.BlockSpec((1, C), lambda i: (0, i)),
                  full((F, H)), full((3*G, H)), full((1, G))],
        out_specs=[pl.BlockSpec((L, C), lambda i: (0, i)), pl.BlockSpec((1, C), lambda i: (0, i))],
        out_shape=[jax.ShapeDtypeStruct((L, N), jnp.float32), jax.ShapeDtypeStruct((1, N), jnp.float32)],
        scratch_shapes=[vb(8*H+16, 256), vb(3*G, H), vm(G, 128), vb(L*H, C), vm(L, C), vm(L, 8, C),
                        vm(2, U, 3*G, C), vm(L, G, C), vm(L, G, C), vm(L // RENORM, G, C), vm(G, C), vm(G, C), vm(L+8, C)],
        compiler_params=pltpu.CompilerParams(vmem_limit_bytes=60*2**20),
        cost_estimate=pl.CostEstimate(flops=6*10**9, bytes_accessed=2**23, transcendentals=4*10**7),
    )(prof, cos, alb, wh, wo.T, sw.reshape(1, G))


def prepare_kernel(cos_ref, alb_ref, keep_ref, ship_ref, count_ref, flags_ref, cos_row_ref, alb_row_ref):
    cos_row_ref[...] = cos_ref[...].astype(jnp.float32).reshape(cos_row_ref.shape)
    alb_row_ref[...] = alb_ref[...].astype(jnp.float32).reshape(alb_row_ref.shape)
    per_peer = flags_ref.shape[0]
    peers = flags_ref.shape[1] // 2
    one_hot = lambda hit: jnp.where(hit, 1.0, 0.0).astype(jnp.bfloat16)
    total = None
    for ref, live_count in ((keep_ref, keep_ref.shape[1]), (ship_ref, count_ref[0])):
        slots = ref[...]
        n = slots.shape[1]
        at = lax.broadcasted_iota(jnp.int32, (per_peer, n), 1)
        share = lax.broadcasted_iota(jnp.int32, (per_peer, n), 0)
        left = one_hot((slots % per_peer == share) & (at < live_count))
        right = one_hot(slots // per_peer == lax.broadcasted_iota(jnp.int32, (peers, n), 0))
        part = lax.dot_general(left, right, (((1,), (1,)), ((), ())), preferred_element_type=jnp.float32)
        total = part if total is None else total + part
    flags_ref[:, :peers] = total
    flags_ref[:, peers:] = jnp.zeros((per_peer, peers), jnp.float32)


def mask_kernel(flags_ref, order_ref, raw_heat_ref, raw_surf_ref, heat_ref, surf_ref):
    columns, peers = flags_ref.shape
    me = lax.axis_index("face") * lax.axis_size("tile") + lax.axis_index("tile")
    one_hot = lambda hit: jnp.where(hit, 1.0, 0.0).astype(jnp.bfloat16)
    contract_lanes = (((1,), (1,)), ((), ()))
    mine = one_hot(lax.broadcasted_iota(jnp.int32, (8, peers), 1) == me)
    flag = lax.dot_general(mine, flags_ref[...].astype(jnp.bfloat16), contract_lanes, preferred_element_type=jnp.float32)
    order = order_ref[...]
    group = lax.broadcasted_iota(jnp.int32, (columns // 128, columns), 0)
    lane = lax.broadcasted_iota(jnp.int32, (128, columns), 0)
    left = jnp.where(order // 128 == group, flag, 0.0).astype(jnp.bfloat16)
    listed = lax.dot_general(left, one_hot(order % 128 == lane), contract_lanes, preferred_element_type=jnp.float32)
    for i in range(columns // 128):
        cs = slice(i * 128, (i + 1) * 128)
        live = listed[i : i + 1, :] > 0.5
        heat_ref[:, cs] = jnp.where(live, raw_heat_ref[:, cs], 0.0)
        surf_ref[:, cs] = jnp.where(live, raw_surf_ref[:, cs], 0.0)


def on_device(profiles, sun_cos, albedo, span_order, keep_list, ship_list, ship_count, w_hidden, optical_weight, solar_weight):
    columns = profiles.shape[0]
    devices = lax.axis_size(("face", "tile"))
    per_peer = columns // devices
    f32 = lambda *s: jax.ShapeDtypeStruct(s, jnp.float32)
    vmem = pl.BlockSpec(memory_space=pltpu.VMEM)
    flags, cos_row, alb_row = pl.pallas_call(
        prepare_kernel,
        in_specs=[vmem] * 4 + [pl.BlockSpec(memory_space=pltpu.SMEM)],
        out_specs=[vmem] * 3,
        out_shape=[f32(per_peer, 2 * devices), f32(1, columns), f32(1, columns)],
        cost_estimate=pl.CostEstimate(flops=2**20, bytes_accessed=2**14, transcendentals=0),
    )(sun_cos, albedo, keep_list, ship_list, ship_count)
    gathered = lax.all_gather(flags, ("face", "tile"), axis=0, tiled=True)
    raw_heat, raw_surf = radiate(profiles, cos_row, alb_row, w_hidden, optical_weight, solar_weight)
    first = pl.BlockSpec((columns, devices), lambda i: (0, 0))
    whole = lambda *s: pl.BlockSpec(s, lambda i: (0, 0))
    heat, surf = pl.pallas_call(
        mask_kernel,
        grid=(1,),
        in_specs=[first, whole(1, columns), whole(*raw_heat.shape), whole(1, columns)],
        out_specs=[whole(*raw_heat.shape), whole(1, columns)],
        out_shape=[f32(*raw_heat.shape), f32(1, columns)],
        cost_estimate=pl.CostEstimate(flops=2**23, bytes_accessed=2**20, transcendentals=0),
    )(gathered, span_order, raw_heat, raw_surf)
    return heat, surf.reshape(-1)


def solution(mesh):
    both = ("face", "tile")
    rows, flat = P(both, None), P(both)
    placed = (rows, flat, flat, rows, rows, rows, flat, P(), P(), P())
    return jax.shard_map(on_device, mesh=mesh, in_specs=placed, out_specs=(P(None, both), flat), check_vma=False)
```

```python
import functools, math
import jax, jax.numpy as jnp
from jax import lax
from jax.experimental import pallas as pl
from jax.experimental.pallas import tpu as pltpu
from jax.sharding import PartitionSpec as P

L, F, H, G = 64, 32, 128, 112
LOG2E = math.log2(math.e)
U = 4
W = 256
DU = 1
ORDER = 0
NODOT = False
STAGE = False
XT = 0
NH = 8
NG = 8
ND = 8
DFIRST = False
RENORM = 8

def radiate_kernel(prof_ref, cos_ref, alb_ref, live_ref, wh_ref, wo_ref, sw_ref, heat_ref, surf_ref,
                   whb, wob, swb, hid, mass_s, k_s, opt, t_s, s_s, inv_s, n_s, d_s, net_s):
    C = prof_ref.shape[0]
    @pl.when(pl.program_id(0) == 0)
    def _():
        whb[...] = jnp.zeros_like(whb)
        wt = (wh_ref[...].astype(jnp.float32) * 0.5).T.astype(jnp.bfloat16)
        for j in range(8):
            whb[j*H:(j+1)*H, j*F:(j+1)*F] = wt
        r = lax.broadcasted_iota(jnp.int32, (16, 256), 0)
        c = lax.broadcasted_iota(jnp.int32, (16, 256), 1)
        whb[8*H:8*H+16, :] = jnp.where(c == r * F, 1.0, 0.0).astype(jnp.bfloat16)
        for g in range(0, G, 16):
            wob[3*g:3*g+16] = wo_ref[g:g+16]
            wob[3*g+16:3*g+32] = (wo_ref[G+g:G+g+16].astype(jnp.float32) * 0.5).astype(jnp.bfloat16)
            wob[3*g+32:3*g+48] = wo_ref[2*G+g:2*G+g+16]
        swb[...] = jnp.broadcast_to(sw_ref[...], (128, G)).T
    cos = cos_ref[...].astype(jnp.float32)
    alb = alb_ref[...].astype(jnp.float32)
    scale = (-2.0 * LOG2E / L) / cos
    n_s[...] = jnp.broadcast_to(alb, (G, C))

    def hidden_chunk(ch, _):
        k0 = pl.multiple_of(ch * 256, 256)
        for s in range(C // W):
            cs = slice(s * W, (s + 1) * W)
            x = prof_ref[cs, pl.ds(k0, 256)]
            if XT == 0:
                pre = lax.dot_general(whb[...], x, (((1,), (1,)), ((), ())), preferred_element_type=jnp.float32)
            elif XT == 1:
                pre = jnp.dot(whb[...], x.T, preferred_element_type=jnp.float32)
            elif XT == 2:
                pre = jnp.dot(whb[...], x.astype(jnp.float32).T.astype(jnp.bfloat16), preferred_element_type=jnp.float32)
            h = pre[:8*H]
            hid[pl.ds(pl.multiple_of(ch * 8 * H, 8 * H), 8 * H), cs] = (h + h * jnp.tanh(h)).astype(jnp.bfloat16)
            mass = pre[8*H:8*H+8]
            mass_s[pl.ds(pl.multiple_of(ch * 8, 8), 8), cs] = mass
            kk = mass * scale[:, cs]
            for j in range(8):
                k_s[ch * 8 + j, :, cs] = jnp.broadcast_to(kk[j:j+1], (8, W))
        return 0
    lax.fori_loop(0, NH, hidden_chunk, 0)

    def dots(l, p):
        for u in range(U):
            for s in range(C // W):
                cs = slice(s * W, (s + 1) * W)
                lu = jnp.maximum(l - u, 0)
                opt[p, u, :, cs] = jnp.dot(wob[...], hid[pl.ds(pl.multiple_of(lu * H, H), H), cs], preferred_element_type=jnp.float32)

    def elem(l, p):
        for s in range(C // 128):
            cs = slice(s * 128, (s + 1) * 128)
            for g in range(0, G, 8):
                base = 3 * (g // 16) * 16 + g % 16
                N = n_s[g:g+8, cs]
                Dn = d_s[g:g+8, cs]
                for u in range(U):
                    a = opt[p, u, base:base+8, cs]
                    b = opt[p, u, base+16:base+24, cs]
                    c = opt[p, u, base+32:base+40, cs]
                    D = jnp.exp2(k_s[l - u, :, cs] * jnp.exp2(a * LOG2E))
                    E = 1.0 - D
                    h2 = (0.245 + 0.245 * jnp.tanh(b)) * E
                    w = h2 * (0.8 * jnp.tanh(c))
                    r = h2 - w
                    t = D + (h2 + w)
                    Dn = Dn - r * N
                    N = r * Dn + t * (t * N)
                    t_s[l - u, g:g+8, cs] = t
                    s_s[l - u, g:g+8, cs] = Dn - N
                n_s[g:g+8, cs] = N
                d_s[g:g+8, cs] = Dn

    dots(L - 1, 0)
    def group(i, _):
        l0 = L - 1 - i * RENORM
        d_s[...] = jnp.ones((G, C), jnp.float32)
        def inner(j, _):
            l = l0 - U * j
            for p in (0, 1):
                @pl.when(lax.rem(j, 2) == p)
                def _():
                    if DFIRST:
                        NODOT or dots(l - U, 1 - p)
                        elem(l, p)
                    else:
                        elem(l, p)
                        NODOT or dots(l - U, 1 - p)
            return 0
        lax.fori_loop(0, RENORM // U, inner, 0)
        ch = L // RENORM - 1 - i
        for g in range(0, G, 8):
            inv = pltpu.reciprocal(d_s[g:g+8, :], approx=False)
            inv_s[ch, g:g+8, :] = inv
            n_s[g:g+8, :] = n_s[g:g+8, :] * inv
        return 0
    lax.fori_loop(0, NG * (8 // RENORM), group, 0)

    V = 128
    for sp in range(C // V):
        cs = slice(sp * V, (sp + 1) * V)
        def down_chunk(ch, down):
            w = list(down)
            rows = []
            for j in range(8):
                l = ch * 8 + j
                if j % RENORM == 0:
                    ii = ch if RENORM == 8 else ch * (8 // RENORM) + j // RENORM
                    w = [w[i] * inv_s[ii, 8*i:8*i+8, cs] for i in range(G // 8)]
                acc = None
                for i in range(G // 8):
                    p = w[i] * s_s[l, 8*i:8*i+8, cs]
                    acc = p if acc is None else acc + p
                    w[i] = w[i] * t_s[l, 8*i:8*i+8, cs]
                rows.append(jnp.sum(acc, axis=0, keepdims=True))
            net_s[pl.ds(pl.multiple_of(ch * 8, 8), 8), cs] = jnp.concatenate(rows, axis=0)
            return tuple(w)
        down = lax.fori_loop(0, ND, down_chunk, tuple(swb[g:g+8, :] * cos[:, cs] for g in range(0, G, 8)))
        acc = down[0]
        for g in range(1, G//8):
            acc = acc + down[g]
        surf = jnp.sum(acc, axis=0, keepdims=True)
        surf_ref[:, cs] = jnp.where(live_ref[:, cs] > 0.5, surf, 0.0)
        net_s[L:L+1, cs] = surf * (1.0 - alb[:, cs])
    live = live_ref[...] > 0.5
    heat_ref[...] = jnp.where(live, L * (net_s[0:L, :] - net_s[1:L+1, :]) / mass_s[...], 0.0)

def radiate(prof, cos, alb, live, wh, wo, sw, C=256):
    N = prof.shape[0]
    grid = (N // C,)
    full = lambda s: pl.BlockSpec(s, lambda i: (0,) * len(s))
    vm = lambda *s: pltpu.VMEM(s, jnp.float32)
    vb = lambda *s: pltpu.VMEM(s, jnp.bfloat16)
    return pl.pallas_call(
        radiate_kernel,
        grid=grid,
        in_specs=[pl.BlockSpec((C, L*F), lambda i: (i, 0)),
                  pl.BlockSpec((1, C), lambda i: (0, i)),
                  pl.BlockSpec((1, C), lambda i: (0, i)),
                  pl.BlockSpec((1, C), lambda i: (0, i)),
                  full((F, H)), full((3*G, H)), full((1, G))],
        out_specs=[pl.BlockSpec((L, C), lambda i: (0, i)), pl.BlockSpec((1, C), lambda i: (0, i))],
        out_shape=[jax.ShapeDtypeStruct((L, N), jnp.float32), jax.ShapeDtypeStruct((1, N), jnp.float32)],
        scratch_shapes=[vb(8*H+16, 256), vb(3*G, H), vm(G, 128), vb(L*H, C), vm(L, C), vm(L, 8, C),
                        vm(2, U, 3*G, C), vm(L, G, C), vm(L, G, C), vm(L // RENORM, G, C), vm(G, C), vm(G, C), vm(L+8, C)],
        compiler_params=pltpu.CompilerParams(vmem_limit_bytes=60*2**20),
        cost_estimate=pl.CostEstimate(flops=6*10**9, bytes_accessed=2**23, transcendentals=4*10**7),
    )(prof, cos, alb, live, wh, wo.T, sw.reshape(1, G))


LO, HI = 16, 8


def listed_kernel(cos_ref, alb_ref, keep_ref, ship_ref, count_ref, order_ref, cos_row_ref, alb_row_ref, live_ref,
                  made, first, turned, second, send1, recv1, send2, recv2):
    per_peer = order_ref.shape[1] // (LO * HI)
    columns = order_ref.shape[1]
    devices = LO * HI
    tiles = lax.axis_size("tile")
    me = lax.axis_index("face") * tiles + lax.axis_index("tile")
    hi, lo = me // LO, me % LO

    def place(h, l):
        device = h * LO + l
        return (device // tiles, device % tiles)

    barrier = pltpu.get_barrier_semaphore()
    for j in range(1, LO):
        pl.semaphore_signal(barrier, inc=1, device_id=place(hi, (lo + j) % LO), device_id_type=pl.DeviceIdType.MESH)
    for j in range(1, HI):
        pl.semaphore_signal(barrier, inc=1, device_id=place((hi + j) % HI, lo), device_id_type=pl.DeviceIdType.MESH)

    cos_row_ref[...] = cos_ref[...].astype(jnp.float32).reshape(cos_row_ref.shape)
    alb_row_ref[...] = alb_ref[...].astype(jnp.float32).reshape(alb_row_ref.shape)
    one_hot = lambda hit: jnp.where(hit, 1.0, 0.0).astype(jnp.bfloat16)
    lanes = (((1,), (1,)), ((), ()))
    total = None
    for ref, live_count in ((keep_ref, keep_ref.shape[1]), (ship_ref, count_ref[...])):
        slots = ref[...]
        n = slots.shape[1]
        row = lax.broadcasted_iota(jnp.int32, (devices, n), 0)
        at = lax.broadcasted_iota(jnp.int32, (devices, n), 1)
        peer = (row % HI) * LO + row // HI
        left = one_hot(slots // per_peer == peer)
        right = one_hot((slots % per_peer == row) & (at < live_count))
        part = lax.dot_general(left, right, lanes, preferred_element_type=jnp.float32)
        total = part if total is None else total + part
    made[...] = total.reshape(LO, HI, 128)

    pl.semaphore_wait(barrier, LO + HI - 2)
    copies = []
    for j in range(1, LO):
        to = (lo + j) % LO
        copy = pltpu.make_async_remote_copy(
            src_ref=made.at[to], dst_ref=first.at[lo], send_sem=send1.at[j], recv_sem=recv1.at[j],
            device_id=place(hi, to), device_id_type=pl.DeviceIdType.MESH)
        copy.start()
        copies.append(copy)
    first[lo] = made[lo]
    for copy in copies:
        copy.wait()
    turned[...] = jnp.swapaxes(first[...], 0, 1)
    copies = []
    for j in range(1, HI):
        to = (hi + j) % HI
        copy = pltpu.make_async_remote_copy(
            src_ref=turned.at[to], dst_ref=second.at[hi], send_sem=send2.at[j], recv_sem=recv2.at[j],
            device_id=place(to, lo), device_id_type=pl.DeviceIdType.MESH)
        copy.start()
        copies.append(copy)
    second[hi] = turned[hi]
    for copy in copies:
        copy.wait()

    got = second[...].reshape(devices, 128).astype(jnp.bfloat16)
    pick = one_hot(lax.broadcasted_iota(jnp.int32, (per_peer, 128), 0) == lax.broadcasted_iota(jnp.int32, (per_peer, 128), 1))
    flags = lax.dot_general(pick, got, lanes, preferred_element_type=jnp.float32).astype(jnp.bfloat16)
    span = lax.broadcasted_iota(jnp.int32, (devices, columns), 0)
    at = lax.broadcasted_iota(jnp.int32, (devices, columns), 1)
    spread = jnp.dot(flags, one_hot(at // per_peer == span), preferred_element_type=jnp.float32)
    share = lax.broadcasted_iota(jnp.int32, (per_peer, columns), 0)
    at8 = lax.broadcasted_iota(jnp.int32, (per_peer, columns), 1)
    flag = jnp.sum(jnp.where(at8 % per_peer == share, spread, 0.0), axis=0, keepdims=True)
    order = order_ref[...]
    group = lax.broadcasted_iota(jnp.int32, (columns // 128, columns), 0)
    lane = lax.broadcasted_iota(jnp.int32, (128, columns), 0)
    placed = jnp.where(order // 128 == group, flag, 0.0).astype(jnp.bfloat16)
    listed = lax.dot_general(placed, one_hot(order % 128 == lane), lanes, preferred_element_type=jnp.float32)
    for i in range(columns // 128):
        live_ref[:, i * 128 : (i + 1) * 128] = listed[i : i + 1, :]


def find_listed(sun_cos, albedo, keep_list, ship_list, ship_count, span_order):
    columns = sun_cos.shape[0]
    row = jax.ShapeDtypeStruct((1, columns), jnp.float32)
    vmem = pl.BlockSpec(memory_space=pltpu.VMEM)
    dma = pltpu.SemaphoreType.DMA
    vm = lambda *s: pltpu.VMEM(s, jnp.float32)
    return pl.pallas_call(
        listed_kernel,
        in_specs=[vmem] * 6,
        out_specs=[vmem] * 3,
        out_shape=[row] * 3,
        scratch_shapes=[vm(LO, HI, 128), vm(LO, HI, 128), vm(HI, LO, 128), vm(HI, LO, 128), dma((LO,)), dma((LO,)), dma((HI,)), dma((HI,))],
        compiler_params=pltpu.CompilerParams(collective_id=0, has_side_effects=True),
        cost_estimate=pl.CostEstimate(flops=2**23, bytes_accessed=2**17, transcendentals=0),
    )(sun_cos, albedo, keep_list, ship_list, ship_count.reshape(1, 1), span_order)


def on_device(profiles, sun_cos, albedo, span_order, keep_list, ship_list, ship_count, w_hidden, optical_weight, solar_weight):
    cos_row, alb_row, live = find_listed(sun_cos, albedo, keep_list, ship_list, ship_count, span_order)
    heat, surf = radiate(profiles, cos_row, alb_row, live, w_hidden, optical_weight, solar_weight)
    return heat, surf.reshape(-1)


def solution(mesh):
    both = ("face", "tile")
    rows, flat = P(both, None), P(both)
    placed = (rows, flat, flat, rows, rows, rows, flat, P(), P(), P())
    return jax.shard_map(on_device, mesh=mesh, in_specs=placed, out_specs=(P(None, both), flat), check_vma=False)
```

```python
import functools, math
import jax, jax.numpy as jnp
from jax import lax
from jax.experimental import pallas as pl
from jax.experimental.pallas import tpu as pltpu
from jax.sharding import PartitionSpec as P

L, F, H, G = 64, 32, 128, 112
LOG2E = math.log2(math.e)
U = 4
W = 256
GT = 16
DFIRST = False
RENORM = 8

LO, HI = 16, 8


def here():
    tiles = lax.axis_size("tile")
    me = lax.axis_index("face") * tiles + lax.axis_index("tile")
    return me // LO, me % LO


def place(h, l):
    tiles = lax.axis_size("tile")
    device = h * LO + l
    return (device // tiles, device % tiles)


def one_hot(hit):
    return jnp.where(hit, 1.0, 0.0).astype(jnp.bfloat16)


LANES = (((1,), (1,)), ((), ()))


def greet():
    hi, lo = here()
    barrier = pltpu.get_barrier_semaphore()
    for j in range(1, LO):
        pl.semaphore_signal(barrier, inc=1, device_id=place(hi, (lo + j) % LO), device_id_type=pl.DeviceIdType.MESH)
    for j in range(1, HI):
        pl.semaphore_signal(barrier, inc=1, device_id=place((hi + j) % HI, lo), device_id_type=pl.DeviceIdType.MESH)


def make_flags(keep_ref, ship_ref, count_ref, made, per_peer):
    devices = LO * HI
    total = None
    for ref, live_count in ((keep_ref, keep_ref.shape[1]), (ship_ref, count_ref[...])):
        slots = ref[...]
        n = slots.shape[1]
        row = lax.broadcasted_iota(jnp.int32, (devices, n), 0)
        at = lax.broadcasted_iota(jnp.int32, (devices, n), 1)
        peer = (row % HI) * LO + row // HI
        left = one_hot(slots // per_peer == peer)
        right = one_hot((slots % per_peer == row) & (at < live_count))
        part = lax.dot_general(left, right, LANES, preferred_element_type=jnp.float32)
        total = part if total is None else total + part
    made[...] = total.reshape(LO, HI, 128)


def first_copies(made, first, send, recv):
    hi, lo = here()
    out = []
    for j in range(1, LO):
        to = (lo + j) % LO
        out.append(pltpu.make_async_remote_copy(
            src_ref=made.at[to], dst_ref=first.at[lo], send_sem=send.at[j], recv_sem=recv.at[j],
            device_id=place(hi, to), device_id_type=pl.DeviceIdType.MESH))
    return out


def second_copies(turned, second, send, recv):
    hi, lo = here()
    out = []
    for j in range(1, HI):
        to = (hi + j) % HI
        out.append(pltpu.make_async_remote_copy(
            src_ref=turned.at[to], dst_ref=second.at[hi], send_sem=send.at[j], recv_sem=recv.at[j],
            device_id=place(to, lo), device_id_type=pl.DeviceIdType.MESH))
    return out


def listed_columns(second, order_ref, per_peer):
    columns = order_ref.shape[1]
    devices = LO * HI
    got = second[...].reshape(devices, 128).astype(jnp.bfloat16)
    pick = one_hot(lax.broadcasted_iota(jnp.int32, (per_peer, 128), 0) == lax.broadcasted_iota(jnp.int32, (per_peer, 128), 1))
    flags = lax.dot_general(pick, got, LANES, preferred_element_type=jnp.float32).astype(jnp.bfloat16)
    span = lax.broadcasted_iota(jnp.int32, (devices, columns), 0)
    at = lax.broadcasted_iota(jnp.int32, (devices, columns), 1)
    spread = jnp.dot(flags, one_hot(at // per_peer == span), preferred_element_type=jnp.float32)
    share = lax.broadcasted_iota(jnp.int32, (per_peer, columns), 0)
    at8 = lax.broadcasted_iota(jnp.int32, (per_peer, columns), 1)
    flag = jnp.sum(jnp.where(at8 % per_peer == share, spread, 0.0), axis=0, keepdims=True)
    order = order_ref[...]
    group = lax.broadcasted_iota(jnp.int32, (columns // 128, columns), 0)
    lane = lax.broadcasted_iota(jnp.int32, (128, columns), 0)
    placed = jnp.where(order // 128 == group, flag, 0.0).astype(jnp.bfloat16)
    listed = lax.dot_general(placed, one_hot(order % 128 == lane), LANES, preferred_element_type=jnp.float32)
    return listed


def radiate_kernel(prof_ref, cos_ref, alb_ref, keep_ref, ship_ref, count_ref, order_ref, wh_ref, wo_ref, sw_ref,
                   heat_ref, surf_ref,
                   whb, wob, swb, hid, mass_s, k_s, opt, t_s, s_s, inv_s, n_s, d_s, net_s, cos_row, alb_row,
                   made, first, turned, second, send1, recv1, send2, recv2):
    C = prof_ref.shape[0]
    step = pl.program_id(0)
    per_peer = order_ref.shape[1] // (LO * HI)
    mine = pl.ds(pl.multiple_of(step * C, C), C)
    @pl.when(step == 0)
    def _():
        greet()
        make_flags(keep_ref, ship_ref, count_ref, made, per_peer)
        cos_row[...] = cos_ref[...].astype(jnp.float32).reshape(cos_row.shape)
        alb_row[...] = alb_ref[...].astype(jnp.float32).reshape(alb_row.shape)
        whb[...] = jnp.zeros_like(whb)
        wt = (wh_ref[...].astype(jnp.float32) * 0.5).T.astype(jnp.bfloat16)
        for j in range(8):
            whb[j*H:(j+1)*H, j*F:(j+1)*F] = wt
        r = lax.broadcasted_iota(jnp.int32, (16, 256), 0)
        c = lax.broadcasted_iota(jnp.int32, (16, 256), 1)
        whb[8*H:8*H+16, :] = jnp.where(c == r * F, 1.0, 0.0).astype(jnp.bfloat16)
        wob[:G] = wo_ref[:G]
        wob[G:2*G] = (wo_ref[G:2*G].astype(jnp.float32) * 0.5).astype(jnp.bfloat16)
        wob[2*G:] = wo_ref[2*G:]
        swb[...] = jnp.broadcast_to(sw_ref[...], (128, G)).T
    cos = cos_row[:, mine]
    alb = alb_row[:, mine]
    scale = (-2.0 * LOG2E / L) / cos
    n_s[...] = jnp.broadcast_to(alb, (G, C))

    def hidden_chunk(ch, _):
        k0 = pl.multiple_of(ch * 256, 256)
        for s in range(C // W):
            cs = slice(s * W, (s + 1) * W)
            x = prof_ref[cs, pl.ds(k0, 256)]
            pre = lax.dot_general(whb[...], x, (((1,), (1,)), ((), ())), preferred_element_type=jnp.float32)
            h = pre[:8*H]
            hid[pl.ds(pl.multiple_of(ch * 8 * H, 8 * H), 8 * H), cs] = (h + h * jnp.tanh(h)).astype(jnp.bfloat16)
            mass = pre[8*H:8*H+8]
            mass_s[pl.ds(pl.multiple_of(ch * 8, 8), 8), cs] = mass
            kk = mass * scale[:, cs]
            for j in range(8):
                k_s[ch * 8 + j, :, cs] = jnp.broadcast_to(kk[j:j+1], (8, W))
        return 0
    lax.fori_loop(0, 8, hidden_chunk, 0)

    def dots(l, p):
        for u in range(U):
            for s in range(C // W):
                cs = slice(s * W, (s + 1) * W)
                lu = jnp.maximum(l - u, 0)
                opt[p, u, :, cs] = jnp.dot(wob[...], hid[pl.ds(pl.multiple_of(lu * H, H), H), cs], preferred_element_type=jnp.float32)

    def elem(l, p):
        for s in range(C // 128):
            cs = slice(s * 128, (s + 1) * 128)
            for g in range(0, G, GT):
                kv = lambda lv: k_s[lv, :, cs] if GT == 8 else jnp.concatenate([k_s[lv, :, cs]] * (GT // 8), axis=0)
                N = n_s[g:g+GT, cs]
                Dn = d_s[g:g+GT, cs]
                for u in range(U):
                    a = opt[p, u, g:g+GT, cs]
                    b = opt[p, u, G+g:G+g+GT, cs]
                    c = opt[p, u, 2*G+g:2*G+g+GT, cs]
                    D = jnp.exp2(kv(l - u) * jnp.exp2(a * LOG2E))
                    E = 1.0 - D
                    h2 = (0.245 + 0.245 * jnp.tanh(b)) * E
                    w = h2 * (0.8 * jnp.tanh(c))
                    r = h2 - w
                    t = D + (h2 + w)
                    Dn = Dn - r * N
                    N = r * Dn + t * (t * N)
                    t_s[l - u, g:g+GT, cs] = t
                    s_s[l - u, g:g+GT, cs] = Dn - N
                n_s[g:g+GT, cs] = N
                d_s[g:g+GT, cs] = Dn

    dots(L - 1, 0)
    def group(i, _):
        l0 = L - 1 - i * RENORM
        d_s[...] = jnp.ones((G, C), jnp.float32)
        def inner(j, _):
            l = l0 - U * j
            for p in (0, 1):
                @pl.when(lax.rem(j, 2) == p)
                def _():
                    if DFIRST:
                        dots(l - U, 1 - p)
                        elem(l, p)
                    else:
                        elem(l, p)
                        dots(l - U, 1 - p)
            return 0
        lax.fori_loop(0, RENORM // U, inner, 0)
        ch = L // RENORM - 1 - i
        for g in range(0, G, 8):
            inv = pltpu.reciprocal(d_s[g:g+8, :], approx=False)
            inv_s[ch, g:g+8, :] = inv
            n_s[g:g+8, :] = n_s[g:g+8, :] * inv
        return 0
    lax.fori_loop(0, 8 * (8 // RENORM), group, 0)

    V = 128
    for sp in range(C // V):
        cs = slice(sp * V, (sp + 1) * V)
        def down_chunk(ch, down):
            w = list(down)
            rows = []
            for j in range(8):
                l = ch * 8 + j
                if j % RENORM == 0:
                    ii = ch if RENORM == 8 else ch * (8 // RENORM) + j // RENORM
                    w = [w[i] * inv_s[ii, 8*i:8*i+8, cs] for i in range(G // 8)]
                acc = None
                for i in range(G // 8):
                    p = w[i] * s_s[l, 8*i:8*i+8, cs]
                    acc = p if acc is None else acc + p
                    w[i] = w[i] * t_s[l, 8*i:8*i+8, cs]
                rows.append(jnp.sum(acc, axis=0, keepdims=True))
            net_s[pl.ds(pl.multiple_of(ch * 8, 8), 8), cs] = jnp.concatenate(rows, axis=0)
            return tuple(w)
        down = lax.fori_loop(0, 8, down_chunk, tuple(swb[g:g+8, :] * cos[:, cs] for g in range(0, G, 8)))
        acc = down[0]
        for g in range(1, G//8):
            acc = acc + down[g]
        surf = jnp.sum(acc, axis=0, keepdims=True)
        surf_ref[:, pl.ds(pl.multiple_of(step * C + sp * V, V), V)] = surf
        net_s[L:L+1, cs] = surf * (1.0 - alb[:, cs])
    heat_ref[:, mine] = L * (net_s[0:L, :] - net_s[1:L+1, :]) / mass_s[...]

    @pl.when(step == 0)
    def _():
        pl.semaphore_wait(pltpu.get_barrier_semaphore(), LO + HI - 2)
        for copy in first_copies(made, first, send1, recv1):
            copy.start()

    @pl.when(step == 1)
    def _():
        hi, lo = here()
        first[lo] = made[lo]
        for copy in first_copies(made, first, send1, recv1):
            copy.wait()
        turned[...] = jnp.swapaxes(first[...], 0, 1)
        for copy in second_copies(turned, second, send2, recv2):
            copy.start()

    @pl.when(step == 2)
    def _():
        hi, lo = here()
        second[hi] = turned[hi]
        for copy in second_copies(turned, second, send2, recv2):
            copy.wait()

    @pl.when(step == pl.num_programs(0) - 1)
    def _():
        listed = listed_columns(second, order_ref, per_peer)
        for i in range(order_ref.shape[1] // 128):
            cs = slice(i * 128, (i + 1) * 128)
            live = listed[i : i + 1, :] > 0.5
            heat_ref[:, cs] = jnp.where(live, heat_ref[:, cs], 0.0)
            surf_ref[:, cs] = jnp.where(live, surf_ref[:, cs], 0.0)


def on_device(profiles, sun_cos, albedo, span_order, keep_list, ship_list, ship_count, w_hidden, optical_weight, solar_weight):
    N, C = profiles.shape[0], 256
    full = lambda *s: pl.BlockSpec(s, lambda i: (0,) * len(s))
    vmem = pl.BlockSpec(memory_space=pltpu.VMEM)
    vm = lambda *s: pltpu.VMEM(s, jnp.float32)
    vb = lambda *s: pltpu.VMEM(s, jnp.bfloat16)
    dma = pltpu.SemaphoreType.DMA
    heat, surf = pl.pallas_call(
        radiate_kernel,
        grid=(N // C,),
        in_specs=[pl.BlockSpec((C, L*F), lambda i: (i, 0)), vmem, vmem, vmem, vmem, vmem, vmem,
                  full(F, H), full(3*G, H), full(1, G)],
        out_specs=[full(L, N), full(1, N)],
        out_shape=[jax.ShapeDtypeStruct((L, N), jnp.float32), jax.ShapeDtypeStruct((1, N), jnp.float32)],
        scratch_shapes=[vb(8*H+16, 256), vb(3*G, H), vm(G, 128), vb(L*H, C), vm(L, C), vm(L, 8, C),
                        vm(2, U, 3*G, C), vm(L, G, C), vm(L, G, C), vm(L // RENORM, G, C), vm(G, C), vm(G, C), vm(L+8, C),
                        vm(1, N), vm(1, N),
                        vm(LO, HI, 128), vm(LO, HI, 128), vm(HI, LO, 128), vm(HI, LO, 128), dma((LO,)), dma((LO,)), dma((HI,)), dma((HI,))],
        compiler_params=pltpu.CompilerParams(vmem_limit_bytes=60*2**20, collective_id=0, has_side_effects=True),
        cost_estimate=pl.CostEstimate(flops=6*10**9, bytes_accessed=2**23, transcendentals=4*10**7),
    )(profiles, sun_cos, albedo, keep_list, ship_list, ship_count.reshape(1, 1), span_order, w_hidden, optical_weight.T, solar_weight.reshape(1, G))
    return heat, surf.reshape(-1)


def solution(mesh):
    both = ("face", "tile")
    rows, flat = P(both, None), P(both)
    placed = (rows, flat, flat, rows, rows, rows, flat, P(), P(), P())
    return jax.shard_map(on_device, mesh=mesh, in_specs=placed, out_specs=(P(None, both), flat), check_vma=False)
```

```python
import functools, math
import jax, jax.numpy as jnp
from jax import lax
from jax.experimental import pallas as pl
from jax.experimental.pallas import tpu as pltpu
from jax.sharding import PartitionSpec as P

L, F, H, G = 64, 32, 128, 112
LOG2E = math.log2(math.e)
U = 4
W = 256
GT = 16
DFIRST = False
RENORM = 8

LO, HI = 16, 8


def here():
    tiles = lax.axis_size("tile")
    me = lax.axis_index("face") * tiles + lax.axis_index("tile")
    return me // LO, me % LO


def place(h, l):
    tiles = lax.axis_size("tile")
    device = h * LO + l
    return (device // tiles, device % tiles)


def one_hot(hit):
    return jnp.where(hit, 1.0, 0.0).astype(jnp.bfloat16)


LANES = (((1,), (1,)), ((), ()))


def greet():
    hi, lo = here()
    barrier = pltpu.get_barrier_semaphore()
    for j in range(1, LO):
        pl.semaphore_signal(barrier, inc=1, device_id=place(hi, (lo + j) % LO), device_id_type=pl.DeviceIdType.MESH)
    for j in range(1, HI):
        pl.semaphore_signal(barrier, inc=1, device_id=place((hi + j) % HI, lo), device_id_type=pl.DeviceIdType.MESH)


def make_flags(keep_ref, ship_ref, count_ref, made, per_peer):
    devices = LO * HI
    total = None
    for ref, live_count in ((keep_ref, keep_ref.shape[1]), (ship_ref, count_ref[...])):
        slots = ref[...]
        n = slots.shape[1]
        row = lax.broadcasted_iota(jnp.int32, (devices, n), 0)
        at = lax.broadcasted_iota(jnp.int32, (devices, n), 1)
        peer = (row % HI) * LO + row // HI
        left = one_hot(slots // per_peer == peer)
        right = one_hot((slots % per_peer == row) & (at < live_count))
        part = lax.dot_general(left, right, LANES, preferred_element_type=jnp.float32)
        total = part if total is None else total + part
    made[...] = total.reshape(LO, HI, 128)


def first_copies(made, first, send, recv):
    hi, lo = here()
    out = []
    for j in range(1, LO):
        to = (lo + j) % LO
        out.append(pltpu.make_async_remote_copy(
            src_ref=made.at[to], dst_ref=first.at[lo], send_sem=send.at[j], recv_sem=recv.at[j],
            device_id=place(hi, to), device_id_type=pl.DeviceIdType.MESH))
    return out


def second_copies(turned, second, send, recv):
    hi, lo = here()
    out = []
    for j in range(1, HI):
        to = (hi + j) % HI
        out.append(pltpu.make_async_remote_copy(
            src_ref=turned.at[to], dst_ref=second.at[hi], send_sem=send.at[j], recv_sem=recv.at[j],
            device_id=place(to, lo), device_id_type=pl.DeviceIdType.MESH))
    return out


def listed_columns(second, order_ref, per_peer):
    columns = order_ref.shape[1]
    devices = LO * HI
    got = second[...].reshape(devices, 128).astype(jnp.bfloat16)
    pick = one_hot(lax.broadcasted_iota(jnp.int32, (per_peer, 128), 0) == lax.broadcasted_iota(jnp.int32, (per_peer, 128), 1))
    flags = lax.dot_general(pick, got, LANES, preferred_element_type=jnp.float32).astype(jnp.bfloat16)
    span = lax.broadcasted_iota(jnp.int32, (devices, columns), 0)
    at = lax.broadcasted_iota(jnp.int32, (devices, columns), 1)
    spread = jnp.dot(flags, one_hot(at // per_peer == span), preferred_element_type=jnp.float32)
    share = lax.broadcasted_iota(jnp.int32, (per_peer, columns), 0)
    at8 = lax.broadcasted_iota(jnp.int32, (per_peer, columns), 1)
    flag = jnp.sum(jnp.where(at8 % per_peer == share, spread, 0.0), axis=0, keepdims=True)
    order = order_ref[...]
    group = lax.broadcasted_iota(jnp.int32, (columns // 128, columns), 0)
    lane = lax.broadcasted_iota(jnp.int32, (128, columns), 0)
    placed = jnp.where(order // 128 == group, flag, 0.0).astype(jnp.bfloat16)
    listed = lax.dot_general(placed, one_hot(order % 128 == lane), LANES, preferred_element_type=jnp.float32)
    return listed


def radiate_kernel(prof_ref, cos_ref, alb_ref, keep_ref, ship_ref, count_ref, order_ref, wh_ref, wo_ref, sw_ref,
                   heat_ref, surf_ref, live_ref,
                   whb, wob, swb, hid, mass_s, k_s, opt, t_s, s_s, inv_s, n_s, d_s, net_s, cos_row, alb_row,
                   made, first, turned, second, send1, recv1, send2, recv2):
    halves, C = prof_ref.shape[0] // W, W
    step = pl.program_id(0)
    per_peer = order_ref.shape[1] // (LO * HI)
    @pl.when(step == 0)
    def _():
        greet()
        make_flags(keep_ref, ship_ref, count_ref, made, per_peer)
        cos_row[...] = cos_ref[...].astype(jnp.float32).reshape(cos_row.shape)
        alb_row[...] = alb_ref[...].astype(jnp.float32).reshape(alb_row.shape)
        whb[...] = jnp.zeros_like(whb)
        wt = (wh_ref[...].astype(jnp.float32) * 0.5).T.astype(jnp.bfloat16)
        for j in range(8):
            whb[j*H:(j+1)*H, j*F:(j+1)*F] = wt
        r = lax.broadcasted_iota(jnp.int32, (16, 256), 0)
        c = lax.broadcasted_iota(jnp.int32, (16, 256), 1)
        whb[8*H:8*H+16, :] = jnp.where(c == r * F, 1.0, 0.0).astype(jnp.bfloat16)
        wob[:G] = wo_ref[:G]
        wob[G:2*G] = (wo_ref[G:2*G].astype(jnp.float32) * 0.5).astype(jnp.bfloat16)
        wob[2*G:] = wo_ref[2*G:]
        swb[...] = jnp.broadcast_to(sw_ref[...], (128, G)).T
    def hidden_chunk(ch, _):
        k0 = pl.multiple_of(ch * 256, 256)
        for s in range(halves):
            x = prof_ref[s * W : (s + 1) * W, pl.ds(k0, 256)]
            pre = lax.dot_general(whb[...], x, (((1,), (1,)), ((), ())), preferred_element_type=jnp.float32)
            h = pre[:8*H]
            hid[s, pl.ds(pl.multiple_of(ch * 8 * H, 8 * H), 8 * H), :] = (h + h * jnp.tanh(h)).astype(jnp.bfloat16)
            mass = pre[8*H:8*H+8]
            mass_s[s, pl.ds(pl.multiple_of(ch * 8, 8), 8), :] = mass
            scale = (-2.0 * LOG2E / L) / cos_row[:, pl.ds(pl.multiple_of((step * halves + s) * W, W), W)]
            kk = mass * scale
            for j in range(8):
                k_s[s, ch * 8 + j] = jnp.broadcast_to(kk[j:j+1], (8, W))
        return 0
    lax.fori_loop(0, 8, hidden_chunk, 0)

    def one_half(half, _):
        q = step * halves + half
        mine = pl.ds(pl.multiple_of(q * C, C), C)
        cos = cos_row[:, mine]
        alb = alb_row[:, mine]
        n_s[...] = jnp.broadcast_to(alb, (G, C))

        def dots(l, p):
            for u in range(U):
                lu = jnp.maximum(l - u, 0)
                opt[p, u] = jnp.dot(wob[...], hid[half, pl.ds(pl.multiple_of(lu * H, H), H), :], preferred_element_type=jnp.float32)

        def elem(l, p):
            for s in range(C // 128):
                cs = slice(s * 128, (s + 1) * 128)
                for g in range(0, G, GT):
                    kv = lambda lv: k_s[half, lv, :, cs] if GT == 8 else jnp.concatenate([k_s[half, lv, :, cs]] * (GT // 8), axis=0)
                    N = n_s[g:g+GT, cs]
                    Dn = d_s[g:g+GT, cs]
                    for u in range(U):
                        a = opt[p, u, g:g+GT, cs]
                        b = opt[p, u, G+g:G+g+GT, cs]
                        c = opt[p, u, 2*G+g:2*G+g+GT, cs]
                        D = jnp.exp2(kv(l - u) * jnp.exp2(a * LOG2E))
                        E = 1.0 - D
                        h2 = (0.245 + 0.245 * jnp.tanh(b)) * E
                        w = h2 * (0.8 * jnp.tanh(c))
                        r = h2 - w
                        t = D + (h2 + w)
                        Dn = Dn - r * N
                        N = r * Dn + t * (t * N)
                        t_s[l - u, g:g+GT, cs] = t
                        s_s[l - u, g:g+GT, cs] = Dn - N
                    n_s[g:g+GT, cs] = N
                    d_s[g:g+GT, cs] = Dn

        dots(L - 1, 0)
        def group(i, _):
            l0 = L - 1 - i * RENORM
            d_s[...] = jnp.ones((G, C), jnp.float32)
            def inner(j, _):
                l = l0 - U * j
                for p in (0, 1):
                    @pl.when(lax.rem(j, 2) == p)
                    def _():
                        if DFIRST:
                            dots(l - U, 1 - p)
                            elem(l, p)
                        else:
                            elem(l, p)
                            dots(l - U, 1 - p)
                return 0
            lax.fori_loop(0, RENORM // U, inner, 0)
            ch = L // RENORM - 1 - i
            for g in range(0, G, 8):
                inv = pltpu.reciprocal(d_s[g:g+8, :], approx=False)
                inv_s[ch, g:g+8, :] = inv
                n_s[g:g+8, :] = n_s[g:g+8, :] * inv
            return 0
        lax.fori_loop(0, 8 * (8 // RENORM), group, 0)

        V = 128
        for sp in range(C // V):
            cs = slice(sp * V, (sp + 1) * V)
            def down_chunk(ch, down):
                w = list(down)
                rows = []
                for j in range(8):
                    l = ch * 8 + j
                    if j % RENORM == 0:
                        ii = ch if RENORM == 8 else ch * (8 // RENORM) + j // RENORM
                        w = [w[i] * inv_s[ii, 8*i:8*i+8, cs] for i in range(G // 8)]
                    acc = None
                    for i in range(G // 8):
                        p = w[i] * s_s[l, 8*i:8*i+8, cs]
                        acc = p if acc is None else acc + p
                        w[i] = w[i] * t_s[l, 8*i:8*i+8, cs]
                    rows.append(jnp.sum(acc, axis=0, keepdims=True))
                net_s[pl.ds(pl.multiple_of(ch * 8, 8), 8), cs] = jnp.concatenate(rows, axis=0)
                return tuple(w)
            down = lax.fori_loop(0, 8, down_chunk, tuple(swb[g:g+8, :] * cos[:, cs] for g in range(0, G, 8)))
            acc = down[0]
            for g in range(1, G//8):
                acc = acc + down[g]
            surf = jnp.sum(acc, axis=0, keepdims=True)
            surf_ref[:, pl.ds(pl.multiple_of(q * C + sp * V, V), V)] = surf
            net_s[L:L+1, cs] = surf * (1.0 - alb[:, cs])
        heat_ref[:, mine] = L * (net_s[0:L, :] - net_s[1:L+1, :]) / mass_s[half]

        @pl.when(q == 0)
        def _():
            pl.semaphore_wait(pltpu.get_barrier_semaphore(), LO + HI - 2)
            for copy in first_copies(made, first, send1, recv1):
                copy.start()

        @pl.when(q == 1)
        def _():
            hi, lo = here()
            first[lo] = made[lo]
            for copy in first_copies(made, first, send1, recv1):
                copy.wait()
            turned[...] = jnp.swapaxes(first[...], 0, 1)
            for copy in second_copies(turned, second, send2, recv2):
                copy.start()

        @pl.when(q == 2)
        def _():
            hi, lo = here()
            second[hi] = turned[hi]
            for copy in second_copies(turned, second, send2, recv2):
                copy.wait()
        return 0

    lax.fori_loop(0, halves, one_half, 0)

    @pl.when(step == pl.num_programs(0) - 1)
    def _():
        listed = listed_columns(second, order_ref, per_peer)
        for i in range(order_ref.shape[1] // 128):
            live_ref[:, i * 128 : (i + 1) * 128] = listed[i : i + 1, :]


def zero_kernel(raw_heat_ref, raw_surf_ref, live_ref, heat_ref, surf_ref):
    live = live_ref[...] > 0.5
    heat_ref[...] = jnp.where(live, raw_heat_ref[...], 0.0)
    surf_ref[...] = jnp.where(live, raw_surf_ref[...], 0.0)


def on_device(profiles, sun_cos, albedo, span_order, keep_list, ship_list, ship_count, w_hidden, optical_weight, solar_weight):
    N, C = profiles.shape[0], 2 * W
    full = lambda *s: pl.BlockSpec(s, lambda i: (0,) * len(s))
    vmem = pl.BlockSpec(memory_space=pltpu.VMEM)
    vm = lambda *s: pltpu.VMEM(s, jnp.float32)
    vb = lambda *s: pltpu.VMEM(s, jnp.bfloat16)
    dma = pltpu.SemaphoreType.DMA
    raw_heat, raw_surf, live = pl.pallas_call(
        radiate_kernel,
        grid=(N // C,),
        in_specs=[pl.BlockSpec((C, L*F), lambda i: (i, 0)), vmem, vmem, vmem, vmem, vmem, vmem,
                  full(F, H), full(3*G, H), full(1, G)],
        out_specs=[full(L, N), full(1, N), full(1, N)],
        out_shape=[jax.ShapeDtypeStruct((n, N), jnp.float32) for n in (L, 1, 1)],
        scratch_shapes=[vb(8*H+16, 256), vb(3*G, H), vm(G, 128), vb(C // W, L*H, W), vm(C // W, L, W), vm(C // W, L, 8, W),
                        vm(2, U, 3*G, W), vm(L, G, W), vm(L, G, W), vm(L // RENORM, G, W), vm(G, W), vm(G, W), vm(L+8, W),
                        vm(1, N), vm(1, N),
                        vm(LO, HI, 128), vm(LO, HI, 128), vm(HI, LO, 128), vm(HI, LO, 128), dma((LO,)), dma((LO,)), dma((HI,)), dma((HI,))],
        compiler_params=pltpu.CompilerParams(vmem_limit_bytes=60*2**20, collective_id=0, has_side_effects=True),
        cost_estimate=pl.CostEstimate(flops=6*10**9, bytes_accessed=2**23, transcendentals=4*10**7),
    )(profiles, sun_cos, albedo, keep_list, ship_list, ship_count.reshape(1, 1), span_order, w_hidden, optical_weight.T, solar_weight.reshape(1, G))
    heat, surf = pl.pallas_call(
        zero_kernel,
        out_shape=[jax.ShapeDtypeStruct((n, N), jnp.float32) for n in (L, 1)],
        cost_estimate=pl.CostEstimate(flops=2**17, bytes_accessed=2**19, transcendentals=0),
    )(raw_heat, raw_surf, live)
    return heat, surf.reshape(-1)


def solution(mesh):
    both = ("face", "tile")
    rows, flat = P(both, None), P(both)
    placed = (rows, flat, flat, rows, rows, rows, flat, P(), P(), P())
    return jax.shard_map(on_device, mesh=mesh, in_specs=placed, out_specs=(P(None, both), flat), check_vma=False)
```
